32 devices in a mesh: tok: 8 (over z, x), head: 4 (over y, core).
Axes of the slice: x: 2, y: 2, z: 4, core: 2. Of those that a mesh axis runs over, the one named last changes fastest.
Arguments:
- queries: bfloat16 [32768, 4, 1024], P('tok', 'head'), as said below
- keys: bfloat16 [32768, 4, 128], P('tok', 'head'), as said below
- basis: float32 [4, 1024, 256], P('head'), may hold values from -0.1875 to 0.1875
Outputs:
- subspace: float32 [4, 1024, 256], P('head')
- keymap: float32 [4, 128, 256], replicated
The draws below stay inside these ranges and needn't reach their ends.
Inputs may be any that keep to these rules, and one draw needn't show every extreme that they name: `queries`: query features are correlated within a group and share a common part with the keys. `keys`: keys share a common part with the queries of the same tokens.
All inputs are finite; a program needn't handle non-finite values.
Results may differ from the reference program's by a relative error of at most 0.0007.
Values sent between devices are 32-bit elements; how exact they have to be, the bound alone decides.
A program may use at most 64 MiB of HBM per device.

```python
import math
import jax
import jax.numpy as jnp
from jax import lax

HD = 128
RANK = 256
GROUPS = 4
QW = 1024
TOKENS = 32768


def shared_part(key):
    latent = jax.random.normal(jax.random.fold_in(key, 7), (TOKENS, 16), jnp.float32)
    rowscale = jnp.exp(jax.random.uniform(jax.random.fold_in(key, 8), (TOKENS, 1, 1), jnp.float32) * math.log(10.0))
    return (latent, rowscale)


def draw_queries(key, part):
    latent, rowscale = shared_part(key)
    noise = jax.random.normal(jax.random.fold_in(key, 1), (TOKENS, GROUPS, QW), jnp.float32)
    colscale = jnp.exp(jax.random.uniform(jax.random.fold_in(key, 3), (1, GROUPS, QW), jnp.float32) * math.log(3.0))
    spread = jnp.repeat(latent, QW // 16, axis=-1)[:, None, :]
    mixed = noise + 0.6 * jnp.roll(noise, 1, axis=-1) + 0.7 * spread
    return (0.5 * mixed * colscale * rowscale).astype(jnp.bfloat16)


def draw_keys(key, part):
    latent, rowscale = shared_part(key)
    noise = jax.random.normal(jax.random.fold_in(key, 4), (TOKENS, GROUPS, HD), jnp.float32)
    spread = jnp.repeat(latent, HD // 16, axis=-1)[:, None, :]
    return ((0.6 * noise + spread) * rowscale * 0.5).astype(jnp.bfloat16)


def levels(key, shape, shards, low, top_value):
    factor_of, own = 1.0, jax.random.fold_in(key, 6)
    for dim, blocks in shards:
        steps = jnp.exp(jax.random.uniform(jax.random.fold_in(own, dim), (blocks,), jnp.float32, low / len(shards), top_value / len(shards)))
        factor_of = factor_of * jnp.repeat(steps, shape[dim] // blocks).reshape([-1 if axis == dim else 1 for axis in range(len(shape))])
    return factor_of


def centred(own_key, shape, scale, bound, pieces=(), held_as=jnp.bfloat16):
    loudness = levels(own_key, shape, pieces, -0.22, 0.18) if pieces else 1.0
    array = jax.random.normal(own_key, shape, jnp.float32) * scale * loudness
    return jnp.minimum(jnp.maximum(array, -bound), bound).astype(held_as)


def setup_inputs(seed: int = 0) -> dict:
    streams_of = jax.random.split(jax.random.key(seed), 4)
    return {
        "queries": draw_queries(jax.random.fold_in(streams_of[3], 71), 0),
        "keys": draw_keys(jax.random.fold_in(streams_of[3], 71), 0),
        "basis": centred(streams_of[2], (GROUPS, QW, RANK), QW ** -0.5, 0.1875, ((0, 4),), jnp.float32),
    }


ridge = 0.1
eps = 1e-06
high = lax.Precision.HIGHEST

def orthonormal(image):
    inner = jnp.dot(image.T, image, precision=high)
    lower = jnp.linalg.cholesky(inner)
    return jax.scipy.linalg.solve_triangular(lower, image.T, lower=True).T

def solve_group(query_rows, key_rows, start_basis):
    gram = jnp.dot(query_rows.T.astype(jnp.float32), query_rows.astype(jnp.float32), preferred_element_type=jnp.float32) / TOKENS
    cross = jnp.dot(key_rows.T.astype(jnp.float32), query_rows.astype(jnp.float32), preferred_element_type=jnp.float32) / TOKENS
    scale = jnp.trace(gram) / gram.shape[0] + eps
    image = jnp.dot(gram, start_basis, precision=high)
    refined = orthonormal(image)
    small = jnp.dot(refined.T, jnp.dot(gram, refined, precision=high), precision=high)
    reduced = small / scale + ridge * jnp.eye(refined.shape[1], dtype=jnp.float32)
    rhs = jnp.dot(cross, refined, precision=high)
    factor = jnp.linalg.cholesky(reduced)
    mapped = jax.scipy.linalg.cho_solve((factor, True), rhs.T).T
    return (refined, mapped)

def reference(queries, keys, basis):
    spaces = []
    maps = []
    for group in range(GROUPS):
        refined, mapped = solve_group(queries[:, group, :], keys[:, group, :], basis[group])
        spaces.append(refined)
        maps.append(mapped)
    return (jnp.stack(spaces), jnp.stack(maps))
```

```python
import jax
import jax.numpy as jnp
from jax import lax
from jax.sharding import PartitionSpec as P

ridge = 0.1
eps = 1e-06
high = lax.Precision.HIGHEST


def orthonormal(image):
    inner = jnp.dot(image.T, image, precision=high)
    lower = jnp.linalg.cholesky(inner)
    return jax.scipy.linalg.solve_triangular(lower, image.T, lower=True).T


def transposed_product(left, right):
    return lax.dot_general(
        left, right, (((0,), (0,)), ((), ())), preferred_element_type=jnp.float32
    )


def on_device(queries, keys, basis):
    query_rows = queries[:, 0, :]
    key_rows = keys[:, 0, :]
    start_basis = basis[0]
    width = query_rows.shape[1]
    rank = start_basis.shape[1]
    total = query_rows.shape[0] * lax.axis_size("tok")
    gram_part = transposed_product(query_rows, query_rows) / total
    cross_part = transposed_product(key_rows, query_rows) / total
    image = lax.psum(jnp.dot(gram_part, start_basis, precision=high), "tok")
    refined = orthonormal(image)
    small_part = jnp.dot(refined.T, jnp.dot(gram_part, refined, precision=high), precision=high)
    rhs_part = jnp.dot(cross_part, refined, precision=high)
    trace_part = jnp.full((8, rank), jnp.trace(gram_part))
    packed = lax.psum(jnp.concatenate([small_part, rhs_part, trace_part], axis=0), "tok")
    small, rhs, trace = packed[:rank], packed[rank:-8], packed[-1, 0]
    scale = trace / width + eps
    reduced = small / scale + ridge * jnp.eye(rank, dtype=jnp.float32)
    factor = jnp.linalg.cholesky(reduced)
    mapped = jax.scipy.linalg.cho_solve((factor, True), rhs.T).T
    every_map = lax.all_gather(mapped[None], "head", axis=0, tiled=True)
    return (refined[None], every_map)


def solution(mesh):
    placed = (P("tok", "head", None), P("tok", "head", None), P("head", None, None))
    return jax.shard_map(
        on_device,
        mesh=mesh,
        in_specs=placed,
        out_specs=(P("head", None, None), P()),
        check_vma=False,
    )
```

```python
import functools

import jax
import jax.numpy as jnp
from jax import lax
from jax.experimental import pallas as pl
from jax.experimental.pallas import tpu as pltpu
from jax.sharding import PartitionSpec as P

ridge = 0.1
eps = 1e-06
high = lax.Precision.HIGHEST
MESH = pl.DeviceIdType.MESH
VMEM = pltpu.VMEM
LIMIT = 56 * 1024 * 1024


def dot(left, right, dims):
    return lax.dot_general(
        left, right, ((dims[:1], dims[1:]), ((), ())), precision=high, preferred_element_type=jnp.float32
    )


def transposed_product(left, right):
    return lax.dot_general(
        left, right, (((0,), (0,)), ((), ())), preferred_element_type=jnp.float32
    )


def sum_kernel(ni, no, chunks, x_ref, o_ref, got_i, acc, got_o, send, recv):
    me = lax.axis_index("tok")
    inner, outer = lax.rem(me, ni), lax.div(me, ni)
    chunk_rows = x_ref.shape[0] // chunks
    inner_rows = chunk_rows // ni
    outer_rows = inner_rows // no
    inner_peers = [outer * ni + lax.rem(inner + d, ni) for d in range(1, ni)]
    outer_peers = [lax.rem(outer + d, no) * ni + inner for d in range(1, no)]

    barrier = pltpu.get_barrier_semaphore()
    for peer in inner_peers + outer_peers:
        pl.semaphore_signal(barrier, inc=1, device_id={"tok": peer}, device_id_type=MESH)
    pl.semaphore_wait(barrier, ni + no - 2)

    def rows(start, size):
        return pl.ds(pl.multiple_of(start, 8), size)

    def copy(c, slot, src, dst, peer):
        return pltpu.make_async_remote_copy(
            src_ref=src,
            dst_ref=dst,
            send_sem=send.at[c, slot],
            recv_sem=recv.at[c, slot],
            device_id={"tok": peer},
            device_id_type=MESH,
        )

    started = []
    first, second, third, fourth = [], [], [], []
    for c in range(chunks):
        base = c * chunk_rows
        mine = []
        for d in range(1, ni):
            to = lax.rem(inner + d, ni)
            one = copy(c, d - 1, x_ref.at[rows(base + to * inner_rows, inner_rows)], got_i.at[c, d - 1], inner_peers[d - 1])
            one.start()
            mine.append(one)
        first.append(mine)
    for c in range(chunks):
        base = c * chunk_rows
        total = x_ref[rows(base + inner * inner_rows, inner_rows)]
        for d in range(1, ni):
            first[c][d - 1].wait_recv()
            total = total + got_i[c, d - 1]
        acc[c] = total
        mine = []
        for d in range(1, no):
            to = lax.rem(outer + d, no)
            one = copy(c, ni - 1 + d - 1, acc.at[c, rows(to * outer_rows, outer_rows)], got_o.at[c, d - 1], outer_peers[d - 1])
            one.start()
            mine.append(one)
        second.append(mine)
    for c in range(chunks):
        place = c * chunk_rows + inner * inner_rows + outer * outer_rows
        total = acc[c, rows(outer * outer_rows, outer_rows)]
        for d in range(1, no):
            second[c][d - 1].wait_recv()
            total = total + got_o[c, d - 1]
        part = o_ref.at[rows(place, outer_rows)]
        part[...] = total
        mine = []
        for d in range(1, no):
            one = copy(c, ni + no - 2 + d - 1, part, part, outer_peers[d - 1])
            one.start()
            mine.append(one)
        third.append(mine)
    for c in range(chunks):
        part = o_ref.at[rows(c * chunk_rows + inner * inner_rows, inner_rows)]
        for one in third[c]:
            one.wait_recv()
        mine = []
        for d in range(1, ni):
            one = copy(c, ni + 2 * no - 3 + d - 1, part, part, inner_peers[d - 1])
            one.start()
            mine.append(one)
        fourth.append(mine)
    for c in range(chunks):
        for one in fourth[c]:
            one.wait_recv()
    for stage in (first, second, third, fourth):
        for mine in stage:
            for one in mine:
                one.wait_send()


def sum_over_tok(array, n, chunks, collective_id):
    ni = 2 if n == 8 else max(d for d in (1, 2, 4, 8) if n % d == 0)
    no = n // ni
    height, lanes = array.shape
    while height % (chunks * n * 8):
        chunks //= 2
    chunk_rows = height // chunks
    copies = 2 * (ni + no - 2)
    return pl.pallas_call(
        functools.partial(sum_kernel, ni, no, chunks),
        out_shape=jax.ShapeDtypeStruct(array.shape, array.dtype),
        in_specs=[pl.BlockSpec(memory_space=VMEM)],
        out_specs=pl.BlockSpec(memory_space=VMEM),
        scratch_shapes=[
            VMEM((chunks, max(ni - 1, 1), chunk_rows // ni, lanes), jnp.float32),
            VMEM((chunks, chunk_rows // ni, lanes), jnp.float32),
            VMEM((chunks, max(no - 1, 1), chunk_rows // n, lanes), jnp.float32),
            pltpu.SemaphoreType.DMA((chunks, copies)),
            pltpu.SemaphoreType.DMA((chunks, copies)),
        ],
        compiler_params=pltpu.CompilerParams(
            collective_id=collective_id, has_side_effects=True, vmem_limit_bytes=LIMIT
        ),
    )(array)


def gather_kernel(n, x_ref, o_ref, send, recv, local):
    me = lax.axis_index("head")
    barrier = pltpu.get_barrier_semaphore()
    peers = [lax.rem(me + d, n) for d in range(1, n)]
    for peer in peers:
        pl.semaphore_signal(barrier, inc=1, device_id={"head": peer}, device_id_type=MESH)
    pl.semaphore_wait(barrier, n - 1)
    sent = []
    for d, peer in enumerate(peers):
        one = pltpu.make_async_remote_copy(
            src_ref=x_ref,
            dst_ref=o_ref.at[me],
            send_sem=send.at[d],
            recv_sem=recv.at[d],
            device_id={"head": peer},
            device_id_type=MESH,
        )
        one.start()
        sent.append(one)
    own = pltpu.make_async_copy(x_ref, o_ref.at[me], local)
    own.start()
    own.wait()
    for one in sent:
        one.wait()


def gather_over_head(array, n, collective_id):
    return pl.pallas_call(
        functools.partial(gather_kernel, n),
        out_shape=jax.ShapeDtypeStruct((n,) + array.shape, array.dtype),
        in_specs=[pl.BlockSpec(memory_space=VMEM)],
        out_specs=pl.BlockSpec(memory_space=VMEM),
        scratch_shapes=[
            pltpu.SemaphoreType.DMA((n - 1,)),
            pltpu.SemaphoreType.DMA((n - 1,)),
            pltpu.SemaphoreType.DMA,
        ],
        compiler_params=pltpu.CompilerParams(
            collective_id=collective_id, has_side_effects=True, vmem_limit_bytes=LIMIT
        ),
    )(array)


def factor_inverse_block(block):
    size, step = 128, 8
    tiles = size // step
    lane = lax.broadcasted_iota(jnp.int32, (step, size), 1)
    sub = lax.broadcasted_iota(jnp.int32, (step, size), 0)
    left = [block[step * i : step * (i + 1), :] for i in range(tiles)]
    right = [jnp.where(lane == sub + step * i, 1.0, 0.0).astype(jnp.float32) for i in range(tiles)]
    result = []

    def row(tile, k):
        return jnp.broadcast_to(tile[k : k + 1, :], (step, size))

    def column(tile, k):
        return jnp.broadcast_to(tile[:, k : k + 1], (step, size))

    for p in range(tiles):
        a, w = left[p], right[p]
        own = [column(a, step * p + k) for k in range(step)]
        done = jnp.zeros((step, size), jnp.float32)
        for k in range(step):
            pivot = row(own[k], k)
            inverse = 1.0 / pivot
            root = lax.rsqrt(pivot)
            root = root * (1.5 - 0.5 * pivot * root * root)
            a_row, w_row = row(a, k), row(w, k)
            done = jnp.where(sub == k, w_row * root, done)
            factor = own[k] * inverse
            for m in range(k + 1, step):
                top = row(own[m], k)
                own[m] = jnp.where(sub == k, top * inverse, own[m] - factor * top)
            a = jnp.where(sub == k, a_row * inverse, a - factor * a_row)
            w = jnp.where(sub == k, w_row * inverse, w - factor * w_row)
        result.append(done)
        a_rows = [row(a, k) for k in range(step)]
        w_rows = [row(w, k) for k in range(step)]
        for i in range(p + 1, tiles):
            old = left[i]
            new_a, new_w = old, right[i]
            for k in range(step):
                multiplier = column(old, step * p + k)
                new_a = new_a - multiplier * a_rows[k]
                new_w = new_w - multiplier * w_rows[k]
            left[i], right[i] = new_a, new_w
    return jnp.concatenate(result, axis=0)


def factor_inverse(matrix):
    half = matrix.shape[0] // 2
    w11 = factor_inverse_block(matrix[:half, :half])
    l21 = dot(matrix[half:, :half], w11, (1, 1))
    w22 = factor_inverse_block(matrix[half:, half:] - dot(l21, l21, (1, 1)))
    w21 = -dot(w22, dot(l21, w11, (1, 0)), (1, 0))
    return w11, w21, w22


def refine_kernel(image_ref, gram_ref, cross_ref, refined_ref, packed_ref, inverse):
    image = image_ref[...]
    rank = image.shape[1]
    half = rank // 2
    w11, w21, w22 = factor_inverse(dot(image, image, (0, 0)))
    inverse[:half, :half] = w11
    inverse[:half, half:] = jnp.zeros_like(w11)
    inverse[half:, :half] = w21
    inverse[half:, half:] = w22
    refined = dot(image, inverse[...], (1, 1))
    refined_ref[...] = refined
    packed_ref[:rank, :] = dot(refined, dot(gram_ref[...], refined, (1, 0)), (0, 0))
    packed_ref[rank:, :] = dot(cross_ref[...], refined, (1, 0))


def solve_kernel(width, packed_ref, trace_ref, map_ref, inverse):
    rank = packed_ref.shape[1]
    half = rank // 2
    scale = trace_ref[...] / width + eps
    row = lax.broadcasted_iota(jnp.int32, (rank, rank), 0)
    col = lax.broadcasted_iota(jnp.int32, (rank, rank), 1)
    reduced = packed_ref[:rank, :] / scale[:1] + jnp.where(row == col, ridge, 0.0)
    w11, w21, w22 = factor_inverse(reduced)
    inverse[:half, :half] = w11
    inverse[:half, half:] = jnp.zeros_like(w11)
    inverse[half:, :half] = w21
    inverse[half:, half:] = w22
    first = dot(packed_ref[rank:, :], inverse[...], (1, 1))
    map_ref[...] = dot(first, inverse[...], (1, 0))


def on_device(queries, keys, basis):
    query_rows = queries[:, 0, :]
    key_rows = keys[:, 0, :]
    start_basis = basis[0]
    width = query_rows.shape[1]
    rank = start_basis.shape[1]
    size = key_rows.shape[1]
    n = lax.axis_size("tok")
    total = query_rows.shape[0] * n
    gram_part = transposed_product(query_rows, query_rows) / total
    cross_part = transposed_product(key_rows, query_rows) / total
    image_part = jnp.dot(gram_part, start_basis, precision=high)
    image = sum_over_tok(image_part, n, 4, 0)
    whole = pl.BlockSpec(memory_space=VMEM)
    refined, packed_part = pl.pallas_call(
        refine_kernel,
        out_shape=(
            jax.ShapeDtypeStruct((width, rank), jnp.float32),
            jax.ShapeDtypeStruct((rank + size, rank), jnp.float32),
        ),
        in_specs=[whole] * 3,
        out_specs=(whole, whole),
        scratch_shapes=[VMEM((rank, rank), jnp.float32)],
        compiler_params=pltpu.CompilerParams(vmem_limit_bytes=LIMIT),
    )(image, gram_part, cross_part)
    extra = n * 8 - (rank + size) % (n * 8)
    trace_part = jnp.full((extra, rank), jnp.trace(gram_part))
    packed = sum_over_tok(jnp.concatenate([packed_part, trace_part], axis=0), n, 1, 1)
    mapped = pl.pallas_call(
        functools.partial(solve_kernel, width),
        out_shape=jax.ShapeDtypeStruct((size, rank), jnp.float32),
        in_specs=[whole] * 2,
        out_specs=whole,
        scratch_shapes=[VMEM((rank, rank), jnp.float32)],
        compiler_params=pltpu.CompilerParams(vmem_limit_bytes=LIMIT),
    )(packed[: rank + size], packed[rank + size : rank + size + 8])
    every_map = gather_over_head(mapped, lax.axis_size("head"), 2)
    return (refined[None], every_map)


def solution(mesh):
    placed = (P("tok", "head", None), P("tok", "head", None), P("head", None, None))
    return jax.shard_map(
        on_device,
        mesh=mesh,
        in_specs=placed,
        out_specs=(P("head", None, None), P()),
        check_vma=False,
    )
```

```python
import functools

import jax
import jax.numpy as jnp
from jax import lax
from jax.experimental import pallas as pl
from jax.experimental.pallas import tpu as pltpu
from jax.sharding import PartitionSpec as P

ridge = 0.1
eps = 1e-06
high = lax.Precision.HIGHEST
MESH = pl.DeviceIdType.MESH
VMEM = pltpu.VMEM
LIMIT = 56 * 1024 * 1024


def dot(left, right, dims):
    return lax.dot_general(
        left, right, ((dims[:1], dims[1:]), ((), ())), precision=high, preferred_element_type=jnp.float32
    )


def transposed_product(left, right):
    return lax.dot_general(
        left, right, (((0,), (0,)), ((), ())), preferred_element_type=jnp.float32
    )


def sum_kernel(ni, no, chunks, x_ref, o_ref, got_i, acc, got_o, send, recv):
    me = lax.axis_index("tok")
    inner, outer = lax.rem(me, ni), lax.div(me, ni)
    chunk_rows = x_ref.shape[0] // chunks
    inner_rows = chunk_rows // ni
    outer_rows = inner_rows // no
    inner_peers = [outer * ni + lax.rem(inner + d, ni) for d in range(1, ni)]
    outer_peers = [lax.rem(outer + d, no) * ni + inner for d in range(1, no)]

    barrier = pltpu.get_barrier_semaphore()
    for peer in inner_peers + outer_peers:
        pl.semaphore_signal(barrier, inc=1, device_id={"tok": peer}, device_id_type=MESH)
    pl.semaphore_wait(barrier, ni + no - 2)

    def rows(start, size):
        return pl.ds(pl.multiple_of(start, 8), size)

    def copy(c, slot, src, dst, peer):
        return pltpu.make_async_remote_copy(
            src_ref=src,
            dst_ref=dst,
            send_sem=send.at[c, slot],
            recv_sem=recv.at[c, slot],
            device_id={"tok": peer},
            device_id_type=MESH,
        )

    first, second, third, fourth = [], [], [], []
    for c in range(chunks):
        base = c * chunk_rows
        mine = []
        for d in range(1, ni):
            to = lax.rem(inner + d, ni)
            one = copy(c, d - 1, x_ref.at[rows(base + to * inner_rows, inner_rows)], got_i.at[c, d - 1], inner_peers[d - 1])
            one.start()
            mine.append(one)
        first.append(mine)

    def scatter_outer(c):
        base = c * chunk_rows
        total = x_ref[rows(base + inner * inner_rows, inner_rows)]
        for d in range(1, ni):
            first[c][d - 1].wait_recv()
            total = total + got_i[c, d - 1]
        acc[c] = total
        mine = []
        for d in range(1, no):
            to = lax.rem(outer + d, no)
            one = copy(c, ni - 1 + d - 1, acc.at[c, rows(to * outer_rows, outer_rows)], got_o.at[c, d - 1], outer_peers[d - 1])
            one.start()
            mine.append(one)
        second.append(mine)

    def gather_outer(c):
        place = c * chunk_rows + inner * inner_rows + outer * outer_rows
        total = acc[c, rows(outer * outer_rows, outer_rows)]
        for d in range(1, no):
            second[c][d - 1].wait_recv()
            total = total + got_o[c, d - 1]
        part = o_ref.at[rows(place, outer_rows)]
        part[...] = total
        mine = []
        for d in range(1, no):
            one = copy(c, ni + no - 2 + d - 1, part, part, outer_peers[d - 1])
            one.start()
            mine.append(one)
        third.append(mine)

    def gather_inner(c):
        part = o_ref.at[rows(c * chunk_rows + inner * inner_rows, inner_rows)]
        for one in third[c]:
            one.wait_recv()
        mine = []
        for d in range(1, ni):
            one = copy(c, ni + 2 * no - 3 + d - 1, part, part, inner_peers[d - 1])
            one.start()
            mine.append(one)
        fourth.append(mine)

    for c in range(chunks + 2):
        if c < chunks:
            scatter_outer(c)
        if 0 <= c - 1 < chunks:
            gather_outer(c - 1)
        if 0 <= c - 2 < chunks:
            gather_inner(c - 2)
    for c in range(chunks):
        for one in fourth[c]:
            one.wait_recv()
    for stage in (first, second, third, fourth):
        for mine in stage:
            for one in mine:
                one.wait_send()


def sum_over_tok(array, n, chunks, collective_id):
    ni = 2 if n == 8 else max(d for d in (1, 2, 4, 8) if n % d == 0)
    no = n // ni
    height, lanes = array.shape
    while height % (chunks * n * 8):
        chunks -= 1
    chunk_rows = height // chunks
    copies = 2 * (ni + no - 2)
    return pl.pallas_call(
        functools.partial(sum_kernel, ni, no, chunks),
        out_shape=jax.ShapeDtypeStruct(array.shape, array.dtype),
        in_specs=[pl.BlockSpec(memory_space=VMEM)],
        out_specs=pl.BlockSpec(memory_space=VMEM),
        scratch_shapes=[
            VMEM((chunks, max(ni - 1, 1), chunk_rows // ni, lanes), jnp.float32),
            VMEM((chunks, chunk_rows // ni, lanes), jnp.float32),
            VMEM((chunks, max(no - 1, 1), chunk_rows // n, lanes), jnp.float32),
            pltpu.SemaphoreType.DMA((chunks, copies)),
            pltpu.SemaphoreType.DMA((chunks, copies)),
        ],
        compiler_params=pltpu.CompilerParams(
            collective_id=collective_id, has_side_effects=True, vmem_limit_bytes=LIMIT
        ),
    )(array)


def gather_kernel(n, x_ref, o_ref, send, recv, local):
    me = lax.axis_index("head")
    barrier = pltpu.get_barrier_semaphore()
    peers = [lax.rem(me + d, n) for d in range(1, n)]
    for peer in peers:
        pl.semaphore_signal(barrier, inc=1, device_id={"head": peer}, device_id_type=MESH)
    pl.semaphore_wait(barrier, n - 1)
    sent = []
    for d, peer in enumerate(peers):
        one = pltpu.make_async_remote_copy(
            src_ref=x_ref,
            dst_ref=o_ref.at[me],
            send_sem=send.at[d],
            recv_sem=recv.at[d],
            device_id={"head": peer},
            device_id_type=MESH,
        )
        one.start()
        sent.append(one)
    own = pltpu.make_async_copy(x_ref, o_ref.at[me], local)
    own.start()
    own.wait()
    for one in sent:
        one.wait()


def gather_over_head(array, n, collective_id):
    return pl.pallas_call(
        functools.partial(gather_kernel, n),
        out_shape=jax.ShapeDtypeStruct((n,) + array.shape, array.dtype),
        in_specs=[pl.BlockSpec(memory_space=VMEM)],
        out_specs=pl.BlockSpec(memory_space=VMEM),
        scratch_shapes=[
            pltpu.SemaphoreType.DMA((n - 1,)),
            pltpu.SemaphoreType.DMA((n - 1,)),
            pltpu.SemaphoreType.DMA,
        ],
        compiler_params=pltpu.CompilerParams(
            collective_id=collective_id, has_side_effects=True, vmem_limit_bytes=LIMIT
        ),
    )(array)


def factor_inverse_block(block):
    size, step = 128, 8
    tiles = size // step
    lane = lax.broadcasted_iota(jnp.int32, (step, size), 1)
    sub = lax.broadcasted_iota(jnp.int32, (step, size), 0)
    left = [block[step * i : step * (i + 1), :] for i in range(tiles)]
    right = [jnp.where(lane == sub + step * i, 1.0, 0.0).astype(jnp.float32) for i in range(tiles)]
    result = []

    def row(tile, k):
        return jnp.broadcast_to(tile[k : k + 1, :], (step, size))

    def column(tile, k):
        return jnp.broadcast_to(tile[:, k : k + 1], (step, size))

    for p in range(tiles):
        a, w = left[p], right[p]
        own = [column(a, step * p + k) for k in range(step)]
        done = jnp.zeros((step, size), jnp.float32)
        for k in range(step):
            pivot = row(own[k], k)
            inverse = 1.0 / pivot
            root = lax.rsqrt(pivot)
            root = root * (1.5 - 0.5 * pivot * root * root)
            a_row, w_row = row(a, k), row(w, k)
            done = jnp.where(sub == k, w_row * root, done)
            factor = own[k] * inverse
            for m in range(k + 1, step):
                top = row(own[m], k)
                own[m] = jnp.where(sub == k, top * inverse, own[m] - factor * top)
            a = jnp.where(sub == k, a_row * inverse, a - factor * a_row)
            w = jnp.where(sub == k, w_row * inverse, w - factor * w_row)
        result.append(done)
        a_rows = [row(a, k) for k in range(step)]
        w_rows = [row(w, k) for k in range(step)]
        for i in range(p + 1, tiles):
            old = left[i]
            new_a, new_w = old, right[i]
            for k in range(step):
                multiplier = column(old, step * p + k)
                new_a = new_a - multiplier * a_rows[k]
                new_w = new_w - multiplier * w_rows[k]
            left[i], right[i] = new_a, new_w
    return jnp.concatenate(result, axis=0)


def factor_inverse(a11, a12, a22, inverse):
    half = a11.shape[0]
    w11 = factor_inverse_block(a11)
    l21 = dot(a12, w11, (0, 1))
    w22 = factor_inverse_block(a22 - dot(l21, l21, (1, 1)))
    inverse[:half, :half] = w11
    inverse[:half, half:] = jnp.zeros_like(w11)
    inverse[half:, :half] = -dot(w22, dot(l21, w11, (1, 0)), (1, 0))
    inverse[half:, half:] = w22


def gram_kernel(total, q_ref, k_ref, basis_ref, gram_ref, cross_ref, image_ref, trace_ref):
    step = pl.program_id(0)
    width = q_ref.shape[1]
    block = 256

    @pl.when(step == 0)
    def _():
        gram_ref[...] = jnp.zeros_like(gram_ref)
        cross_ref[...] = jnp.zeros_like(cross_ref)

    for at in range(0, width, block):
        gram_ref[at : at + block, at:] += transposed_product(q_ref[:, at : at + block], q_ref[:, at:])
    cross_ref[...] += transposed_product(k_ref[...], q_ref[...])

    @pl.when(step == pl.num_programs(0) - 1)
    def _():
        cross_ref[...] = cross_ref[...] / total
        row = lax.broadcasted_iota(jnp.int32, (block, block), 0)
        col = lax.broadcasted_iota(jnp.int32, (block, block), 1)
        trace = jnp.zeros((), jnp.float32)
        for at in range(0, width, block):
            gram_ref[at : at + block, at:] = gram_ref[at : at + block, at:] / total
            trace += jnp.sum(jnp.where(row == col, gram_ref[at : at + block, at : at + block], 0.0))
            for to in range(at + block, width, block):
                gram_ref[to : to + block, at : at + block] = gram_ref[at : at + block, to : to + block].T
        trace_ref[...] = jnp.full(trace_ref.shape, trace)
        for at in range(0, width, block):
            image_ref[at : at + block, :] = dot(gram_ref[at : at + block, :], basis_ref[...], (1, 0))


def refine_kernel(image_ref, gram_ref, cross_ref, trace_ref, refined_ref, packed_ref, inverse):
    image = image_ref[...]
    rank = image.shape[1]
    half = rank // 2
    size = cross_ref.shape[0]
    inner = dot(image, image, (0, 0))
    factor_inverse(inner[:half, :half], inner[:half, half:], inner[half:, half:], inverse)
    refined = dot(image, inverse[...], (1, 1))
    refined_ref[...] = refined
    small = dot(refined, dot(gram_ref[...], refined, (1, 0)), (0, 0))
    packed_ref[:half, :] = small[:half]
    packed_ref[half:rank, half:] = small[half:, half:]
    packed_ref[half:rank, :half] = jnp.broadcast_to(trace_ref[:1, :half], (half, half))
    packed_ref[rank : rank + size, :] = dot(cross_ref[...], refined, (1, 0))
    if packed_ref.shape[0] > rank + size:
        packed_ref[rank + size :, :] = jnp.zeros((packed_ref.shape[0] - rank - size, rank), jnp.float32)


def solve_kernel(width, packed_ref, map_ref, inverse):
    rank = packed_ref.shape[1]
    half = rank // 2
    scale = packed_ref[half : half + 1, :half] / width + eps
    row = lax.broadcasted_iota(jnp.int32, (half, half), 0)
    col = lax.broadcasted_iota(jnp.int32, (half, half), 1)
    shift = jnp.where(row == col, ridge, 0.0)
    factor_inverse(
        packed_ref[:half, :half] / scale + shift,
        packed_ref[:half, half:] / scale,
        packed_ref[half:rank, half:] / scale + shift,
        inverse,
    )
    first = dot(packed_ref[rank : rank + map_ref.shape[0], :], inverse[...], (1, 1))
    map_ref[...] = dot(first, inverse[...], (1, 0))


def on_device(queries, keys, basis):
    query_rows = queries[:, 0, :]
    key_rows = keys[:, 0, :]
    start_basis = basis[0]
    width = query_rows.shape[1]
    rank = start_basis.shape[1]
    size = key_rows.shape[1]
    n = lax.axis_size("tok")
    total = query_rows.shape[0] * n
    tokens = query_rows.shape[0]
    block = 1024 if tokens % 1024 == 0 else tokens
    whole = pl.BlockSpec(memory_space=VMEM)
    params = pltpu.CompilerParams(vmem_limit_bytes=LIMIT)
    shape = lambda *dims: jax.ShapeDtypeStruct(dims, jnp.float32)
    fixed = lambda *dims: pl.BlockSpec(dims, lambda i: (0, 0))
    gram_part, cross_part, image_part, trace_part = pl.pallas_call(
        functools.partial(gram_kernel, total),
        grid=(tokens // block,),
        out_shape=(shape(width, width), shape(size, width), shape(width, rank), shape(8, 128)),
        in_specs=[
            pl.BlockSpec((block, width), lambda i: (i, 0)),
            pl.BlockSpec((block, size), lambda i: (i, 0)),
            fixed(width, rank),
        ],
        out_specs=(fixed(width, width), fixed(size, width), fixed(width, rank), fixed(8, 128)),
        compiler_params=params,
    )(query_rows, key_rows, start_basis)
    image = sum_over_tok(image_part, n, 8, 0)
    height = -(-(rank + size) // (8 * n)) * 8 * n
    refined, packed_part = pl.pallas_call(
        refine_kernel,
        out_shape=(shape(width, rank), shape(height, rank)),
        in_specs=[whole] * 4,
        out_specs=(whole, whole),
        scratch_shapes=[VMEM((rank, rank), jnp.float32)],
        compiler_params=params,
    )(image, gram_part, cross_part, trace_part)
    packed = sum_over_tok(packed_part, n, 3, 1)
    mapped = pl.pallas_call(
        functools.partial(solve_kernel, width),
        out_shape=shape(size, rank),
        in_specs=[whole],
        out_specs=whole,
        scratch_shapes=[VMEM((rank, rank), jnp.float32)],
        compiler_params=params,
    )(packed)
    every_map = gather_over_head(mapped, lax.axis_size("head"), 2)
    return (refined[None], every_map)


def solution(mesh):
    placed = (P("tok", "head", None), P("tok", "head", None), P("head", None, None))
    return jax.shard_map(
        on_device,
        mesh=mesh,
        in_specs=placed,
        out_specs=(P("head", None, None), P()),
        check_vma=False,
    )
```
